32 devices in a mesh: ctx: 8 (over z, y), fsdp: 4 (over x, core).
Axes of the slice: x: 2, y: 2, z: 4, core: 2. Of those that a mesh axis runs over, the one named last changes fastest.
Arguments:
- tokens: bfloat16 [4, 1024, 640], P('fsdp', 'ctx'), may hold values from -8 to 8
- positions: int32 [4, 1024], P('fsdp'), may hold values from 0 to 1023, as said below
- qkv_weight: bfloat16 [640, 1536], P('fsdp'), may hold values from -1 to 1
- out_weight: bfloat16 [1024, 640], P('fsdp'), may hold values from -0.1875 to 0.1875
- gate_up_weight: bfloat16 [640, 4096], P('fsdp'), may hold values from -0.25 to 0.25
- down_weight: bfloat16 [2048, 640], P('fsdp'), may hold values from -0.125 to 0.125
- norm_gains: float32 [4, 640], replicated, may hold values from -0.5 to 0.5
- qk_gains: float32 [2, 256], replicated, may hold values from -0.5 to 0.5
- cotangent: bfloat16 [4, 1024, 640], P('fsdp', 'ctx'), may hold values from -6 to 6
Outputs:
- output: float32 [4, 1024, 640], P('fsdp', 'ctx')
- grad_tokens: float32 [4, 1024, 640], P('fsdp', 'ctx')
- grad_qkv: float32 [640, 1536], P('fsdp')
- grad_out: float32 [1024, 640], P('fsdp')
- grad_gate_up: float32 [640, 4096], P('fsdp')
- grad_down: float32 [2048, 640], P('fsdp')
- grad_norm_gains: float32 [4, 640], replicated
- grad_qk_gains: float32 [2, 256], replicated
The draws below stay inside these ranges and needn't reach their ends.
Inputs may be any that keep to these rules, and one draw needn't show every extreme that they name: In every sequence each position 0 to 1023 occurs once. Each device's 2 * 64 stored tokens along ctx are two whole blocks of 64 consecutive positions starting at multiples of 64: block b and block 2 * 8 - 1 - b, in either order.
All inputs are finite; a program needn't handle non-finite values.
Results may differ from the reference program's by a relative error of at most 0.018.
Values may be sent and summed in bfloat16 or wider, within the bound.
A program may use at most 128 MiB of HBM per device.

```python
import math
import jax
import jax.numpy as jnp
from jax import lax

D = 640
NH = 4
HD = 256
FF = 2048
BLK = 64
LENGTH = 1024
SEQS = 4


def draw_tokens(key, part):
    shape = (SEQS, LENGTH, D)
    drawn = jnp.clip(jax.random.normal(key, shape, jnp.float32), -6.0, 6.0)
    return drawn.astype(jnp.bfloat16)


def draw_positions(key, part):
    block_count = LENGTH // BLK
    pair_count = block_count // 2

    def one_sequence(seq_index):
        seq_key = jax.random.fold_in(key, seq_index)
        first_key, second_key = jax.random.split(seq_key)
        pair_order = jax.random.permutation(first_key, pair_count).astype(jnp.int32)
        flipped = jax.random.randint(second_key, (pair_count,), 0, 2)
        early_block = pair_order
        late_block = block_count - 1 - pair_order
        lead_block = jnp.where(flipped == 1, late_block, early_block)
        trail_block = jnp.where(flipped == 1, early_block, late_block)
        blocks = jnp.stack([lead_block, trail_block], 1)
        offsets = jnp.arange(BLK, dtype=jnp.int32)
        return (blocks[:, :, None] * BLK + offsets[None, None, :]).reshape(LENGTH).astype(jnp.int32)
    return jax.vmap(one_sequence)(jnp.arange(SEQS, dtype=jnp.int32))


def draw_qkv_weight(key, part):
    columns = NH * HD + 2 * HD
    spread = D ** (-0.5)
    drawn = jnp.clip(jax.random.normal(key, (D, columns), jnp.float32) * spread, -4.0 * spread, 4.0 * spread)
    return drawn.astype(jnp.bfloat16)


def draw_qk_gains(key, part):
    drawn = jnp.clip(0.25 * jax.random.normal(key, (2, HD), jnp.float32), -0.5, 0.5)
    return drawn


def level_of(own_key, dims, cuts, least, high):
    def one(axis_at, parts):
        draws = jax.random.uniform(jax.random.fold_in(jax.random.fold_in(own_key, 6), axis_at), (parts,), jnp.float32, least / len(cuts), high / len(cuts))
        return jnp.repeat(jnp.exp(draws), dims[axis_at] // parts).reshape((-1,) + (1,) * (len(dims) - axis_at - 1))

    gain = one(*cuts[0])
    for cut in cuts[1:]:
        gain = gain * one(*cut)
    return gain


def bell_draw(stream_key, shape, width, reach, cuts=(), kind=jnp.bfloat16):
    result = jax.random.normal(stream_key, shape, jnp.float32) * width
    if len(cuts) > 0:
        result = level_of(stream_key, shape, cuts, -0.22, 0.18) * result
    return jnp.clip(result, min=-reach, max=reach).astype(kind)


def setup_inputs(seed: int = 0) -> dict:
    key_list = jax.random.split(jax.random.key(seed), 10)
    tokens = draw_tokens(jax.random.fold_in(key_list[9], 71), 0)
    positions = draw_positions(jax.random.fold_in(key_list[9], 71), 0)
    qkv_weight = draw_qkv_weight(jax.random.fold_in(key_list[9], 71), 0)
    out_weight = bell_draw(key_list[3], (NH * HD, D), (NH * HD) ** -0.5, 0.1875, ((0, 4),))
    gate_up_weight = bell_draw(key_list[4], (D, 2 * FF), D ** -0.5, 0.25, ((0, 4),))
    down_weight = bell_draw(key_list[5], (FF, D), FF ** -0.5, 0.125, ((0, 4),))
    norm_gains = jnp.clip(jax.random.uniform(key_list[6], (4, D), jnp.float32, -0.5, 0.5), -0.5, 0.5)
    qk_gains = draw_qk_gains(jax.random.fold_in(key_list[9], 71), 0)
    cotangent = bell_draw(key_list[8], (SEQS, LENGTH, D), 1.0, 6.0, ((0, 4), (1, 8)))
    return dict(tokens=tokens, positions=positions, qkv_weight=qkv_weight, out_weight=out_weight, gate_up_weight=gate_up_weight, down_weight=down_weight, norm_gains=norm_gains, qk_gains=qk_gains, cotangent=cotangent)


EPS = 1e-06
ROPE_BASE = 1000000.0
NEG = -1e+30

def rms_forward(entries, weight):
    inv_rms = lax.rsqrt(lax.optimization_barrier(jnp.mean(entries * entries, axis=-1, keepdims=True)) + EPS)
    return (entries * inv_rms * (1.0 + weight), inv_rms)

def rms_backward(entries, inv_rms, weight, incoming):
    normed = entries * inv_rms
    scaled = incoming * (1.0 + weight)
    lead_axes = tuple(range(incoming.ndim - 1))
    d_weight = lax.optimization_barrier(jnp.sum(incoming * normed, axis=lead_axes))
    d_entries = inv_rms * (scaled - normed * lax.optimization_barrier(jnp.mean(scaled * normed, axis=-1, keepdims=True)))
    return (d_entries, d_weight)

def rope_tables(places, head_size):
    half_size = head_size // 2
    frequency = ROPE_BASE ** (-2.0 * jnp.arange(half_size, dtype=jnp.float32) / head_size)
    angles = places.astype(jnp.float32)[:, None] * frequency[None, :]
    cosine = jnp.cos(angles)
    sine_part = jnp.sin(angles)
    return (jnp.concatenate([cosine, cosine], -1), jnp.concatenate([sine_part, sine_part], -1))

def rotate(entries, cosine, sine_part):
    half_size = entries.shape[-1] // 2
    turned = jnp.concatenate([-entries[..., half_size:], entries[..., :half_size]], -1)
    return entries * cosine + turned * sine_part

def gelu_tanh(entries):
    return jax.nn.gelu(entries, approximate=True)

def attention_forward(query_b, key_b, value_b, places):
    length = key_b.shape[0]
    block_size = math.gcd(length, 512)
    keys_f = key_b.astype(jnp.float32)
    values_f = value_b.astype(jnp.float32)

    def one_block(block_start):
        query_rows = lax.dynamic_slice_in_dim(query_b, block_start, block_size, 0).astype(jnp.float32)
        row_places = lax.dynamic_slice_in_dim(places, block_start, block_size, 0)
        scores = jnp.einsum('thd,ud->thu', query_rows, keys_f)
        visible = places[None, None, :] <= row_places[:, None, None]
        scores = jnp.where(visible, scores, NEG)
        row_peak = lax.optimization_barrier(jnp.max(scores, axis=-1, keepdims=True))
        row_total = lax.optimization_barrier(jnp.sum(jnp.exp(scores - row_peak), axis=-1, keepdims=True))
        row_log = row_peak + jnp.log(row_total)
        probs_b = lax.optimization_barrier(jnp.exp(scores - row_log).astype(jnp.bfloat16))
        mixed_rows = jnp.einsum('thu,ud->thd', probs_b.astype(jnp.float32), values_f)
        return (mixed_rows, row_log[..., 0])
    block_starts = jnp.arange(length // block_size, dtype=jnp.int32) * block_size
    mixed_all, log_all = lax.map(one_block, block_starts)
    return (mixed_all.reshape(length, NH, HD), log_all.reshape(length, NH))

def attention_backward(query_b, key_b, value_b, places, d_mixed_b, log_total, row_delta):
    length = key_b.shape[0]
    block_size = math.gcd(length, 512)
    keys_f = key_b.astype(jnp.float32)
    values_f = value_b.astype(jnp.float32)

    def one_block(carry_grads, block_start):
        key_grad, value_grad = carry_grads
        query_rows = lax.dynamic_slice_in_dim(query_b, block_start, block_size, 0).astype(jnp.float32)
        grad_rows = lax.dynamic_slice_in_dim(d_mixed_b, block_start, block_size, 0).astype(jnp.float32)
        row_places = lax.dynamic_slice_in_dim(places, block_start, block_size, 0)
        row_log = lax.dynamic_slice_in_dim(log_total, block_start, block_size, 0)
        row_dlt = lax.dynamic_slice_in_dim(row_delta, block_start, block_size, 0)
        scores = jnp.einsum('thd,ud->thu', query_rows, keys_f)
        visible = places[None, None, :] <= row_places[:, None, None]
        probs_f = jnp.where(visible, jnp.exp(scores - row_log[..., None]), 0.0)
        probs_b = lax.optimization_barrier(probs_f.astype(jnp.bfloat16)).astype(jnp.float32)
        value_grad = value_grad + jnp.einsum('thu,thd->ud', probs_b, grad_rows)
        grad_probs = jnp.einsum('thd,ud->thu', grad_rows, values_f)
        grad_scores = lax.optimization_barrier((probs_f * (grad_probs - row_dlt[..., None])).astype(jnp.bfloat16)).astype(jnp.float32)
        query_grad = jnp.einsum('thu,ud->thd', grad_scores, keys_f)
        key_grad = key_grad + jnp.einsum('thu,thd->ud', grad_scores, query_rows)
        return ((key_grad, value_grad), query_grad)
    block_starts = jnp.arange(length // block_size, dtype=jnp.int32) * block_size
    zero_grads = (jnp.zeros((length, HD), jnp.float32), jnp.zeros((length, HD), jnp.float32))
    (key_grad, value_grad), query_grads = lax.scan(one_block, zero_grads, block_starts)
    return (query_grads.reshape(length, NH, HD), key_grad, value_grad)

def reference(tokens, positions, qkv_weight, out_weight, gate_up_weight, down_weight, norm_gains, qk_gains, cotangent):
    query_width = NH * HD
    head_scale = HD ** (-0.5)

    def one_sequence(totals, seq_items):
        seq_tokens, seq_places, seq_grad = seq_items
        inputs_f = seq_tokens.astype(jnp.float32)
        normed_in, inv_in = rms_forward(inputs_f, norm_gains[0])
        normed_in_b = normed_in.astype(jnp.bfloat16)
        projected = jnp.dot(normed_in_b, qkv_weight, preferred_element_type=jnp.float32)
        query_pre = projected[:, :query_width].reshape(-1, NH, HD)
        key_pre = projected[:, query_width:query_width + HD]
        value_b = projected[:, query_width + HD:].astype(jnp.bfloat16)
        cosine, sine_part = rope_tables(seq_places, HD)
        query_norm, inv_query = rms_forward(query_pre, qk_gains[0])
        key_norm, inv_key = rms_forward(key_pre, qk_gains[1])
        query_b = (rotate(query_norm, cosine[:, None, :], sine_part[:, None, :]) * head_scale).astype(jnp.bfloat16)
        key_b = rotate(key_norm, cosine, sine_part).astype(jnp.bfloat16)
        mixed_f, log_total = attention_forward(query_b, key_b, value_b, seq_places)
        mixed_b = mixed_f.astype(jnp.bfloat16).reshape(-1, query_width)
        attn_out = jnp.dot(mixed_b, out_weight, preferred_element_type=jnp.float32)
        attn_norm, inv_attn = rms_forward(attn_out, norm_gains[1])
        resid = inputs_f + attn_norm
        normed_ff, inv_ff = rms_forward(resid, norm_gains[2])
        normed_ff_b = normed_ff.astype(jnp.bfloat16)
        gate_up = jnp.dot(normed_ff_b, gate_up_weight, preferred_element_type=jnp.float32)
        gate_part = gate_up[:, :FF]
        up_part = gate_up[:, FF:]
        activated, gelu_pull = jax.vjp(gelu_tanh, gate_part)
        hidden_b = (activated * up_part).astype(jnp.bfloat16)
        ffn_out = jnp.dot(hidden_b, down_weight, preferred_element_type=jnp.float32)
        ffn_norm, inv_out = rms_forward(ffn_out, norm_gains[3])
        output = resid + ffn_norm
        grad_f = seq_grad.astype(jnp.float32)
        d_ffn, gain_three = rms_backward(ffn_out, inv_out, norm_gains[3], grad_f)
        d_ffn_b = d_ffn.astype(jnp.bfloat16)
        grad_down = jnp.dot(hidden_b.T, d_ffn_b, preferred_element_type=jnp.float32)
        d_hidden = jnp.dot(d_ffn_b, down_weight.T, preferred_element_type=jnp.float32)
        d_gate = gelu_pull(d_hidden * up_part)[0]
        d_gate_up_b = jnp.concatenate([d_gate, d_hidden * activated], 1).astype(jnp.bfloat16)
        grad_gate_up = jnp.dot(normed_ff_b.T, d_gate_up_b, preferred_element_type=jnp.float32)
        d_normed_ff = jnp.dot(d_gate_up_b, gate_up_weight.T, preferred_element_type=jnp.float32)
        d_resid_part, gain_two = rms_backward(resid, inv_ff, norm_gains[2], d_normed_ff)
        d_resid = grad_f + d_resid_part
        d_attn, gain_one = rms_backward(attn_out, inv_attn, norm_gains[1], d_resid)
        d_attn_b = d_attn.astype(jnp.bfloat16)
        grad_out = jnp.dot(mixed_b.T, d_attn_b, preferred_element_type=jnp.float32)
        d_mixed_b = jnp.dot(d_attn_b, out_weight.T, preferred_element_type=jnp.float32).astype(jnp.bfloat16)
        d_mixed_heads = d_mixed_b.reshape(-1, NH, HD)
        row_delta = lax.optimization_barrier(jnp.sum(d_mixed_heads.astype(jnp.float32) * mixed_b.reshape(-1, NH, HD).astype(jnp.float32), axis=-1))
        d_query, d_key, d_value = attention_backward(query_b, key_b, value_b, seq_places, d_mixed_heads, log_total, row_delta)
        d_query_norm = rotate(d_query * head_scale, cosine[:, None, :], -sine_part[:, None, :])
        d_query_pre, gain_query = rms_backward(query_pre, inv_query, qk_gains[0], d_query_norm)
        d_key_norm = rotate(d_key, cosine, -sine_part)
        d_key_pre, gain_key = rms_backward(key_pre, inv_key, qk_gains[1], d_key_norm)
        d_projected_b = jnp.concatenate([d_query_pre.reshape(-1, query_width), d_key_pre, d_value], 1).astype(jnp.bfloat16)
        grad_qkv = jnp.dot(normed_in_b.T, d_projected_b, preferred_element_type=jnp.float32)
        d_normed_in = jnp.dot(d_projected_b, qkv_weight.T, preferred_element_type=jnp.float32)
        d_inputs, gain_zero = rms_backward(inputs_f, inv_in, norm_gains[0], d_normed_in)
        grad_tokens = d_resid + d_inputs
        gains_grad = jnp.stack([gain_zero, gain_one, gain_two, gain_three], 0)
        qk_grad = jnp.stack([gain_query, gain_key], 0)
        fresh = (grad_qkv, grad_out, grad_gate_up, grad_down, gains_grad, qk_grad)
        totals = tuple((old_sum + new_sum for old_sum, new_sum in zip(totals, fresh)))
        return (totals, (output, grad_tokens))
    zero_totals = (jnp.zeros((D, query_width + 2 * HD), jnp.float32), jnp.zeros((query_width, D), jnp.float32), jnp.zeros((D, 2 * FF), jnp.float32), jnp.zeros((FF, D), jnp.float32), jnp.zeros((4, D), jnp.float32), jnp.zeros((2, HD), jnp.float32))
    totals, (outputs, grads_in) = lax.scan(one_sequence, zero_totals, (tokens, positions, cotangent))
    return (outputs, grads_in, totals[0], totals[1], totals[2], totals[3], totals[4], totals[5])
```

```python
import functools

import jax
import jax.numpy as jnp
from jax import lax
from jax.experimental import pallas as pl
from jax.experimental.pallas import tpu as pltpu
from jax.sharding import PartitionSpec as P

EPS = 1e-06
ROPE_BASE = 1000000.0
NEG = -1e30
BF = jnp.bfloat16
F32 = jnp.float32
MESH = pl.DeviceIdType.MESH
VMEM_LIMIT = 60 * 1024 * 1024


def rms_forward(entries, weight):
    inv_rms = lax.rsqrt(jnp.mean(entries * entries, axis=-1, keepdims=True) + EPS)
    return (entries * inv_rms * (1.0 + weight), inv_rms)


def rms_backward(entries, inv_rms, weight, incoming):
    normed = entries * inv_rms
    scaled = incoming * (1.0 + weight)
    lead_axes = tuple(range(incoming.ndim - 1))
    d_weight = jnp.sum(incoming * normed, axis=lead_axes)
    d_entries = inv_rms * (scaled - normed * jnp.mean(scaled * normed, axis=-1, keepdims=True))
    return (d_entries, d_weight)


def rope_tables(places, head_size):
    half_size = head_size // 2
    frequency = ROPE_BASE ** (-2.0 * jnp.arange(half_size, dtype=jnp.float32) / head_size)
    angles = places.astype(jnp.float32)[:, None] * frequency[None, :]
    cosine = jnp.cos(angles)
    sine_part = jnp.sin(angles)
    return (jnp.concatenate([cosine, cosine], -1), jnp.concatenate([sine_part, sine_part], -1))


def rotate(entries, cosine, sine_part):
    half_size = entries.shape[-1] // 2
    turned = jnp.concatenate([-entries[..., half_size:], entries[..., :half_size]], -1)
    return entries * cosine + turned * sine_part


def gelu_tanh(entries):
    return jax.nn.gelu(entries, approximate=True)


def nt(left, right):
    return lax.dot_general(left, right, (((1,), (1,)), ((), ())), preferred_element_type=F32)


def tn(left, right):
    return lax.dot_general(left, right, (((0,), (0,)), ((), ())), preferred_element_type=F32)


def nn(left, right):
    return jnp.dot(left, right, preferred_element_type=F32)


class Place:
    def __init__(self, zn):
        ctx, fsdp = lax.axis_index("ctx"), lax.axis_index("fsdp")
        self.zn = zn
        self.z, self.y = ctx // 2, lax.rem(ctx, 2)
        self.x, self.c = fsdp // 2, lax.rem(fsdp, 2)
        self.ctx, self.fsdp = ctx, fsdp
        self.core_peer = (ctx, self.x * 2 + 1 - self.c)
        self.x_peer = (ctx, (1 - self.x) * 2 + self.c)
        self.y_peer = (self.z * 2 + 1 - self.y, fsdp)

    def z_index(self, step):
        return lax.rem(self.z + step, self.zn)

    def z_peer(self, step):
        return (self.z_index(step) * 2 + self.y, self.fsdp)


def greet(peers):
    barrier = pltpu.get_barrier_semaphore()
    for peer in peers:
        pl.semaphore_signal(barrier, inc=1, device_id=peer, device_id_type=MESH)
    pl.semaphore_wait(barrier, len(peers))


class Sender:
    def __init__(self, send_sem, recv_sem):
        self.send_sem, self.recv_sem = send_sem, recv_sem
        self.used = 0
        self.copies = []

    def start(self, source, target, peer):
        slot = self.used
        self.used += 1
        copy = pltpu.make_async_remote_copy(
            src_ref=source,
            dst_ref=target,
            send_sem=self.send_sem.at[slot],
            recv_sem=self.recv_sem.at[slot],
            device_id=peer,
            device_id_type=MESH,
        )
        copy.start()
        self.copies.append(copy)
        return copy

    def finish(self):
        for copy in self.copies:
            copy.wait_send()


def rows_at(start, size):
    return pl.ds(pl.multiple_of(start, 16), size)


def gather_kernel(plan, count, zn, *refs):
    ins, outs = refs[:count], refs[count : 2 * count]
    send_sem, recv_sem, own_sem = refs[2 * count :]
    here = Place(zn)
    greet([here.core_peer, here.x_peer, here.y_peer])
    sender = Sender(send_sem, recv_sem)
    own_copies = []
    state = {}

    def spot(chunk, quarter, half):
        index, col, width = chunk
        rows = ins[index].shape[0]
        if half is None:
            return outs[index].at[rows_at(quarter * rows, rows), pl.ds(col, width)]
        return outs[index].at[
            rows_at(quarter * rows + half * (rows // 2), rows // 2), pl.ds(col, width)
        ]

    def stage(level, at):
        chunk = plan[at]
        index, col, width = chunk
        rows = ins[index].shape[0]
        far = (1 - here.x) * 2 + here.c
        if level == 0:
            half = ins[index].at[rows_at(here.y * (rows // 2), rows // 2), pl.ds(col, width)]
            whole = ins[index].at[:, pl.ds(col, width)]
            to_x = sender.start(half, spot(chunk, here.fsdp, here.y), here.x_peer)
            to_core = sender.start(whole, spot(chunk, here.fsdp, None), here.core_peer)
            own = pltpu.make_async_copy(whole, spot(chunk, here.fsdp, None), own_sem.at[at])
            own.start()
            own_copies.append(own)
            state[at] = [to_x, to_core]
        elif level == 1:
            state[at][0].wait_recv()
            block = spot(chunk, far, here.y)
            state[at].append(sender.start(block, block, here.y_peer))
            state[at].append(sender.start(block, block, here.core_peer))
        elif level == 2:
            state[at][2].wait_recv()
            block = spot(chunk, far, 1 - here.y)
            state[at].append(sender.start(block, block, here.core_peer))
        else:
            for part in (1, 3, 4):
                state[at][part].wait_recv()

    for at in range(len(plan)):
        stage(0, at)
    for tick in range(len(plan) + 2):
        for level in (3, 2, 1):
            at = tick - (level - 1)
            if 0 <= at < len(plan):
                stage(level, at)
    for own in own_copies:
        own.wait()
    sender.finish()


def gather_weights(arrays, zn):
    plan = []
    for index, array in enumerate(arrays):
        width = array.shape[1]
        step = width if width <= 1536 else 1024
        plan += [(index, col, step) for col in range(0, width, step)]
    count = len(arrays)
    return pl.pallas_call(
        functools.partial(gather_kernel, plan, count, zn),
        out_shape=[
            jax.ShapeDtypeStruct((4 * array.shape[0], array.shape[1]), array.dtype)
            for array in arrays
        ],
        in_specs=[pl.BlockSpec(memory_space=pltpu.VMEM)] * count,
        out_specs=[pl.BlockSpec(memory_space=pltpu.VMEM)] * count,
        scratch_shapes=[
            pltpu.SemaphoreType.DMA((5 * len(plan),)),
            pltpu.SemaphoreType.DMA((5 * len(plan),)),
            pltpu.SemaphoreType.DMA((len(plan),)),
        ],
        compiler_params=pltpu.CompilerParams(
            collective_id=0, has_side_effects=True, vmem_limit_bytes=VMEM_LIMIT
        ),
    )(*arrays)


def kv_gather_kernel(zn, in_ref, out_ref, send_sem, recv_sem, own_sem):
    here = Place(zn)
    greet([here.y_peer] + [here.z_peer(step) for step in range(1, zn)])
    sender = Sender(send_sem, recv_sem)
    along_z = [
        sender.start(in_ref, out_ref.at[here.ctx], here.z_peer(step)) for step in range(1, zn)
    ]
    along_y = [sender.start(in_ref, out_ref.at[here.ctx], here.y_peer)]
    own = pltpu.make_async_copy(in_ref, out_ref.at[here.ctx], own_sem.at[0])
    own.start()
    for step in range(1, zn):
        along_z[step - 1].wait_recv()
        block = out_ref.at[here.z_index(zn - step) * 2 + here.y]
        along_y.append(sender.start(block, block, here.y_peer))
    for copy in along_y:
        copy.wait_recv()
    own.wait()
    sender.finish()


def gather_kv(block, zn):
    return pl.pallas_call(
        functools.partial(kv_gather_kernel, zn),
        out_shape=jax.ShapeDtypeStruct((2 * zn,) + block.shape, block.dtype),
        in_specs=[pl.BlockSpec(memory_space=pltpu.VMEM)],
        out_specs=pl.BlockSpec(memory_space=pltpu.VMEM),
        scratch_shapes=[
            pltpu.SemaphoreType.DMA((2 * zn - 1,)),
            pltpu.SemaphoreType.DMA((2 * zn - 1,)),
            pltpu.SemaphoreType.DMA((1,)),
        ],
        compiler_params=pltpu.CompilerParams(
            collective_id=1, has_side_effects=True, vmem_limit_bytes=VMEM_LIMIT
        ),
    )(block)


def kv_reduce_kernel(zn, in_ref, out_ref, from_y, summed, from_z, send_sem, recv_sem):
    here = Place(zn)
    greet([here.y_peer] + [here.z_peer(step) for step in range(1, zn)])
    sender = Sender(send_sem, recv_sem)
    order = list(range(1, zn)) + [0]
    along_y = []
    for step in order:
        target = here.z_index(step)
        along_y.append(
            sender.start(in_ref.at[target * 2 + 1 - here.y], from_y.at[target], here.y_peer)
        )
    along_z = []
    for at, step in enumerate(order):
        along_y[at].wait_recv()
        target = here.z_index(step)
        both = in_ref[target * 2 + here.y].astype(F32) + from_y[target].astype(F32)
        if step == 0:
            out_ref[...] = both
        else:
            summed[step - 1] = both.astype(BF)
            along_z.append(
                sender.start(summed.at[step - 1], from_z.at[step - 1], here.z_peer(step))
            )
    for step in range(1, zn):
        along_z[step - 1].wait_recv()
        out_ref[...] += from_z[step - 1].astype(F32)
    sender.finish()


def reduce_kv(blocks, zn):
    shape = blocks.shape[1:]
    return pl.pallas_call(
        functools.partial(kv_reduce_kernel, zn),
        out_shape=jax.ShapeDtypeStruct(shape, F32),
        in_specs=[pl.BlockSpec(memory_space=pltpu.VMEM)],
        out_specs=pl.BlockSpec(memory_space=pltpu.VMEM),
        scratch_shapes=[
            pltpu.VMEM((zn,) + shape, BF),
            pltpu.VMEM((zn - 1,) + shape, BF),
            pltpu.VMEM((zn - 1,) + shape, BF),
            pltpu.SemaphoreType.DMA((2 * zn - 1,)),
            pltpu.SemaphoreType.DMA((2 * zn - 1,)),
        ],
        compiler_params=pltpu.CompilerParams(
            collective_id=2, has_side_effects=True, vmem_limit_bytes=VMEM_LIMIT
        ),
    )(blocks)


PER_CHUNK = 11


def reduce_kernel(plan, count, zn, *refs):
    ins, small_in = refs[:count], refs[count]
    outs, small_out = refs[count + 1 : 2 * count + 1], refs[2 * count + 1]
    rest = refs[2 * count + 2 :]
    buffers = [rest[5 * at : 5 * at + 5] for at in range(len(plan))]
    small_recv, small_sum, small_z, send_sem, recv_sem = rest[5 * len(plan) :]
    here = Place(zn)
    greet(
        [here.core_peer, here.x_peer, here.y_peer] + [here.z_peer(step) for step in range(1, zn)]
    )
    sender = Sender(send_sem, recv_sem)
    state = {}
    own = here.fsdp
    away = (1 - here.x) * 2 + here.c

    def piece(chunk, z_at):
        index, row, rows, col, width, by_rows = chunk
        half = rows // 2
        if by_rows:
            return (z_at * (half // zn), half // zn, 0, width)
        return (0, half, z_at * (width // zn), width // zn)

    def cut(ref, chunk, z_at, row_base, col_base):
        r0, rows, c0, width = piece(chunk, z_at)
        return ref.at[
            rows_at(row_base + r0, rows), pl.ds(pl.multiple_of(col_base + c0, 128), width)
        ]

    def block(ref, chunk, quarter):
        index, row, rows, col, width, by_rows = chunk
        whole = ref.shape[0] // 4
        return ref.at[rows_at(quarter * whole + row, rows), pl.ds(col, width)]

    def stage(level, at):
        chunk = plan[at]
        index, row, rows, col, width, by_rows = chunk
        from_core, from_x, total, from_y, from_z = buffers[at]
        half = rows // 2
        mine = rows_at(here.y * half, half)
        other = rows_at((1 - here.y) * half, half)
        if level == 0:
            order = (1 - here.x, here.x)
            state[at] = [
                sender.start(
                    block(ins[index], chunk, side * 2 + 1 - here.c),
                    from_core.at[side],
                    here.core_peer,
                )
                for side in (0, 1)
            ]
        elif level == 1:
            for copy in state[at]:
                copy.wait_recv()
            side = 1 - here.x
            from_core[side] = (
                block(ins[index], chunk, away)[...].astype(F32) + from_core[side].astype(F32)
            ).astype(BF)
            state[at] = [sender.start(from_core.at[side], from_x, here.x_peer)]
        elif level == 2:
            state[at][0].wait_recv()
            total[...] = (
                block(ins[index], chunk, own)[...].astype(F32)
                + from_core[here.x].astype(F32)
                + from_x[...].astype(F32)
            ).astype(BF)
            state[at] = [sender.start(total.at[other], from_y, here.y_peer)]
        elif level == 3:
            state[at][0].wait_recv()
            total[mine] = (total[mine].astype(F32) + from_y[...].astype(F32)).astype(BF)
            state[at] = [
                sender.start(
                    cut(total, chunk, here.z_index(step), here.y * half, 0),
                    from_z.at[step - 1],
                    here.z_peer(step),
                )
                for step in range(1, zn)
            ]
        elif level == 4:
            for copy in state[at]:
                copy.wait_recv()
            result = cut(total, chunk, here.z, here.y * half, 0)[...].astype(F32)
            for step in range(1, zn):
                result = result + from_z[step - 1].astype(F32)
            place = cut(outs[index], chunk, here.z, row + here.y * half, col)
            place[...] = result.astype(BF)
            state[at] = [sender.start(place, place, here.z_peer(step)) for step in range(1, zn)]
        elif level == 5:
            for copy in state[at]:
                copy.wait_recv()
            place = outs[index].at[rows_at(row + here.y * half, half), pl.ds(col, width)]
            state[at] = [sender.start(place, place, here.y_peer)]
        else:
            state[at][0].wait_recv()

    def small_stage(level):
        if level == 0:
            state["s"] = [sender.start(small_in, small_recv.at[0], here.core_peer)]
        elif level in (1, 2):
            state["s"][0].wait_recv()
            base = small_in if level == 1 else small_sum.at[0]
            small_sum[level - 1] = base[...] + small_recv[level - 1]
            peer = here.x_peer if level == 1 else here.y_peer
            state["s"] = [sender.start(small_sum.at[level - 1], small_recv.at[level], peer)]
        elif level == 3:
            state["s"][0].wait_recv()
            small_z[here.z] = small_sum[1] + small_recv[2]
            state["s"] = [
                sender.start(small_z.at[here.z], small_z.at[here.z], here.z_peer(step))
                for step in range(1, zn)
            ]
        elif level == 4:
            for copy in state["s"]:
                copy.wait_recv()
            result = small_z[0]
            for z_at in range(1, zn):
                result = result + small_z[z_at]
            small_out[...] = result

    for tick in range(len(plan) + 6):
        for level in range(6, -1, -1):
            at = tick - level
            if 0 <= at < len(plan):
                stage(level, at)
        if tick < 5:
            small_stage(tick)
    sender.finish()


def reduce_plan(arrays, zn):
    plan = []
    for index, array in enumerate(arrays):
        rows, width = array.shape[0] // 4, array.shape[1]
        if width % (128 * zn) == 0:
            step = 1024 if width % 1024 == 0 else 512 if width % 512 == 0 else width
            plan += [(index, 0, rows, col, step, False) for col in range(0, width, step)]
        else:
            step = 256 if rows % 256 == 0 else rows
            plan += [(index, row, step, 0, width, True) for row in range(0, rows, step)]
    return plan


def reduce_weights(arrays, small, zn):
    plan = reduce_plan(arrays, zn)
    count = len(arrays)
    scratch = []
    for index, row, rows, col, width, by_rows in plan:
        half = rows // 2
        z_shape = (half // zn, width) if by_rows else (half, width // zn)
        scratch += [
            pltpu.VMEM((2, rows, width), BF),
            pltpu.VMEM((rows, width), BF),
            pltpu.VMEM((rows, width), BF),
            pltpu.VMEM((half, width), BF),
            pltpu.VMEM((zn - 1,) + z_shape, BF),
        ]
    copies = len(plan) * (5 + 2 * (zn - 1)) + 3 + zn - 1
    return pl.pallas_call(
        functools.partial(reduce_kernel, plan, count, zn),
        out_shape=[
            jax.ShapeDtypeStruct((array.shape[0] // 4, array.shape[1]), array.dtype)
            for array in arrays
        ]
        + [jax.ShapeDtypeStruct(small.shape, small.dtype)],
        in_specs=[pl.BlockSpec(memory_space=pltpu.VMEM)] * (count + 1),
        out_specs=[pl.BlockSpec(memory_space=pltpu.VMEM)] * (count + 1),
        scratch_shapes=scratch
        + [
            pltpu.VMEM((3,) + small.shape, F32),
            pltpu.VMEM((2,) + small.shape, F32),
            pltpu.VMEM((zn,) + small.shape, F32),
            pltpu.SemaphoreType.DMA((copies,)),
            pltpu.SemaphoreType.DMA((copies,)),
        ],
        compiler_params=pltpu.CompilerParams(
            collective_id=3, has_side_effects=True, vmem_limit_bytes=VMEM_LIMIT
        ),
    )(*arrays, small)


def shards(
    ctx_count,
    fsdp_count,
    tokens,
    positions,
    qkv_weight,
    out_weight,
    gate_up_weight,
    down_weight,
    norm_gains,
    qk_gains,
    cotangent,
):
    zn = ctx_count // 2
    own_kernels = fsdp_count == 4 and ctx_count == 8
    row_count = tokens.shape[1]
    all_places = positions[0]
    length = all_places.shape[0]
    places = lax.dynamic_slice_in_dim(all_places, lax.axis_index("ctx") * row_count, row_count, 0)
    weights = (qkv_weight, out_weight, gate_up_weight, down_weight)
    if own_kernels:
        qkv_full, out_full, gate_up_full, down_full = gather_weights(weights, zn)
    else:
        qkv_full, out_full, gate_up_full, down_full = [
            lax.all_gather(weight, "fsdp", axis=0, tiled=True) for weight in weights
        ]
    head_size = qk_gains.shape[1]
    query_width = out_full.shape[0]
    head_count = query_width // head_size
    hidden_size = down_full.shape[0]
    head_scale = head_size ** (-0.5)
    inputs_f = tokens[0].astype(F32)
    normed_in, inv_in = rms_forward(inputs_f, norm_gains[0])
    normed_in_b = normed_in.astype(BF)
    projected = nn(normed_in_b, qkv_full)
    query_pre = projected[:, :query_width].reshape(row_count, head_count, head_size)
    query_pre = query_pre.transpose(1, 0, 2)
    key_pre = projected[:, query_width : query_width + head_size]
    value_b = projected[:, query_width + head_size :].astype(BF)
    cosine, sine_part = rope_tables(places, head_size)
    query_norm, inv_query = rms_forward(query_pre, qk_gains[0])
    key_norm, inv_key = rms_forward(key_pre, qk_gains[1])
    query_b = (rotate(query_norm, cosine, sine_part) * head_scale).astype(BF)
    key_b = rotate(key_norm, cosine, sine_part).astype(BF)
    kv_b = jnp.concatenate([key_b, value_b], 1)
    if own_kernels:
        kv_all = gather_kv(kv_b, zn).reshape(length, 2 * head_size)
    else:
        kv_all = lax.all_gather(kv_b, "ctx", axis=0, tiled=True)
    key_all, value_all = kv_all[:, :head_size], kv_all[:, head_size:]
    query_rows = query_b.reshape(head_count * row_count, head_size)
    row_places = jnp.tile(places, head_count)
    visible = all_places[None, :] <= row_places[:, None]
    scores = jnp.where(visible, nt(query_rows, key_all), NEG)
    row_peak = jnp.max(scores, axis=1, keepdims=True)
    log_total = row_peak + jnp.log(jnp.sum(jnp.exp(scores - row_peak), axis=1, keepdims=True))
    probs_f = jnp.exp(scores - log_total)
    probs_b = probs_f.astype(BF)
    mixed_rows = nn(probs_b, value_all).astype(BF)

    def heads_in(rows):
        return rows.reshape(head_count, row_count, head_size)

    mixed_b = heads_in(mixed_rows).transpose(1, 0, 2).reshape(row_count, query_width)
    attn_out = nn(mixed_b, out_full)
    attn_norm, inv_attn = rms_forward(attn_out, norm_gains[1])
    resid = inputs_f + attn_norm
    normed_ff, inv_ff = rms_forward(resid, norm_gains[2])
    normed_ff_b = normed_ff.astype(BF)
    gate_up = nn(normed_ff_b, gate_up_full)
    gate_part = gate_up[:, :hidden_size]
    up_part = gate_up[:, hidden_size:]
    activated, gelu_pull = jax.vjp(gelu_tanh, gate_part)
    hidden_b = (activated * up_part).astype(BF)
    ffn_out = nn(hidden_b, down_full)
    ffn_norm, inv_out = rms_forward(ffn_out, norm_gains[3])
    output = resid + ffn_norm
    grad_f = cotangent[0].astype(F32)
    d_ffn, gain_three = rms_backward(ffn_out, inv_out, norm_gains[3], grad_f)
    d_ffn_b = d_ffn.astype(BF)
    grad_down_full = tn(hidden_b, d_ffn_b).astype(BF)
    d_hidden = nt(d_ffn_b, down_full)
    d_gate = gelu_pull(d_hidden * up_part)[0]
    d_gate_up_b = jnp.concatenate([d_gate, d_hidden * activated], 1).astype(BF)
    grad_gate_up_full = tn(normed_ff_b, d_gate_up_b).astype(BF)
    d_normed_ff = nt(d_gate_up_b, gate_up_full)
    d_resid_part, gain_two = rms_backward(resid, inv_ff, norm_gains[2], d_normed_ff)
    d_resid = grad_f + d_resid_part
    d_attn, gain_one = rms_backward(attn_out, inv_attn, norm_gains[1], d_resid)
    d_attn_b = d_attn.astype(BF)
    grad_out_full = tn(mixed_b, d_attn_b).astype(BF)
    d_mixed_b = nt(d_attn_b, out_full).astype(BF)
    d_mixed_rows = d_mixed_b.reshape(row_count, head_count, head_size).transpose(1, 0, 2)
    d_mixed_rows = d_mixed_rows.reshape(head_count * row_count, head_size)
    row_delta = jnp.sum(
        d_mixed_rows.astype(F32) * mixed_rows.astype(F32), axis=-1, keepdims=True
    )
    value_acc = tn(probs_b, d_mixed_rows)
    grad_probs = nt(d_mixed_rows, value_all)
    grad_scores = (probs_f * (grad_probs - row_delta)).astype(BF)
    d_query = heads_in(nn(grad_scores, key_all))
    key_acc = tn(grad_scores, query_rows)
    kv_acc = jnp.concatenate([key_acc, value_acc], 1)
    if own_kernels:
        kv_grad = reduce_kv(kv_acc.astype(BF).reshape(2 * zn, row_count, 2 * head_size), zn)
    else:
        kv_grad = lax.psum_scatter(kv_acc, "ctx", scatter_dimension=0, tiled=True)
    d_query_norm = rotate(d_query * head_scale, cosine, -sine_part)
    d_query_pre, gain_query = rms_backward(query_pre, inv_query, qk_gains[0], d_query_norm)
    d_key_norm = rotate(kv_grad[:, :head_size], cosine, -sine_part)
    d_key_pre, gain_key = rms_backward(key_pre, inv_key, qk_gains[1], d_key_norm)
    d_query_flat = d_query_pre.transpose(1, 0, 2).reshape(row_count, query_width)
    d_projected_b = jnp.concatenate([d_query_flat, d_key_pre, kv_grad[:, head_size:]], 1)
    d_projected_b = d_projected_b.astype(BF)
    grad_qkv_full = tn(normed_in_b, d_projected_b).astype(BF)
    d_normed_in = nt(d_projected_b, qkv_full)
    d_inputs, gain_zero = rms_backward(inputs_f, inv_in, norm_gains[0], d_normed_in)
    grad_tokens = d_resid + d_inputs
    gains_local = jnp.stack([gain_zero, gain_one, gain_two, gain_three], 0)
    qk_local = jnp.stack([gain_query, gain_key], 0)
    grads = (grad_down_full, grad_gate_up_full, grad_out_full, grad_qkv_full)
    if own_kernels:
        wide = norm_gains.shape[1] - head_size
        small = jnp.concatenate(
            [gains_local, jnp.pad(qk_local, ((0, 2), (0, wide)))], 0
        )
        grad_down, grad_gate_up, grad_out, grad_qkv, small = reduce_weights(grads, small, zn)
        gains_total, qk_total = small[:4], small[4:6, :head_size]
    else:
        parts = [lax.psum_scatter(grad, "fsdp", scatter_dimension=0, tiled=True) for grad in grads]
        parts = lax.psum([part.astype(F32) for part in parts], "ctx")
        grad_down, grad_gate_up, grad_out, grad_qkv = parts
        gains_total, qk_total = lax.psum((gains_local, qk_local), ("ctx", "fsdp"))
    return (
        output[None],
        grad_tokens[None],
        grad_qkv.astype(F32),
        grad_out.astype(F32),
        grad_gate_up.astype(F32),
        grad_down.astype(F32),
        gains_total,
        qk_total,
    )


def solution(mesh):
    in_specs = (
        P("fsdp", "ctx", None),
        P("fsdp", None),
        P("fsdp", None),
        P("fsdp", None),
        P("fsdp", None),
        P("fsdp", None),
        P(),
        P(),
        P("fsdp", "ctx", None),
    )
    out_specs = (
        P("fsdp", "ctx", None),
        P("fsdp", "ctx", None),
        P("fsdp", None),
        P("fsdp", None),
        P("fsdp", None),
        P("fsdp", None),
        P(),
        P(),
    )
    body = functools.partial(shards, mesh.shape["ctx"], mesh.shape["fsdp"])
    return jax.shard_map(body, mesh=mesh, in_specs=in_specs, out_specs=out_specs, check_vma=False)
```

```python
import functools

import jax
import jax.numpy as jnp
from jax import lax
from jax.experimental import pallas as pl
from jax.experimental.pallas import tpu as pltpu
from jax.sharding import PartitionSpec as P

EPS = 1e-06
ROPE_BASE = 1000000.0
NEG = -1e30
BF = jnp.bfloat16
F32 = jnp.float32
MESH = pl.DeviceIdType.MESH
VMEM_LIMIT = 60 * 1024 * 1024


def rms_forward(entries, weight):
    inv_rms = lax.rsqrt(jnp.mean(entries * entries, axis=-1, keepdims=True) + EPS)
    return (entries * inv_rms * (1.0 + weight), inv_rms)


def rms_backward(entries, inv_rms, weight, incoming):
    normed = entries * inv_rms
    scaled = incoming * (1.0 + weight)
    lead_axes = tuple(range(incoming.ndim - 1))
    d_weight = jnp.sum(incoming * normed, axis=lead_axes)
    d_entries = inv_rms * (scaled - normed * jnp.mean(scaled * normed, axis=-1, keepdims=True))
    return (d_entries, d_weight)


def rope_tables(places, head_size):
    half_size = head_size // 2
    frequency = ROPE_BASE ** (-2.0 * jnp.arange(half_size, dtype=jnp.float32) / head_size)
    angles = places.astype(jnp.float32)[:, None] * frequency[None, :]
    cosine = jnp.cos(angles)
    sine_part = jnp.sin(angles)
    return (jnp.concatenate([cosine, cosine], -1), jnp.concatenate([sine_part, sine_part], -1))


def rotate(entries, cosine, sine_part):
    half_size = entries.shape[-1] // 2
    turned = jnp.concatenate([-entries[..., half_size:], entries[..., :half_size]], -1)
    return entries * cosine + turned * sine_part


def gelu_tanh(entries):
    return jax.nn.gelu(entries, approximate=True)


def nt(left, right):
    return lax.dot_general(left, right, (((1,), (1,)), ((), ())), preferred_element_type=F32)


def tn(left, right):
    return lax.dot_general(left, right, (((0,), (0,)), ((), ())), preferred_element_type=F32)


def nn(left, right):
    return jnp.dot(left, right, preferred_element_type=F32)


class Place:
    def __init__(self, zn):
        ctx, fsdp = lax.axis_index("ctx"), lax.axis_index("fsdp")
        self.zn = zn
        self.z, self.y = ctx // 2, lax.rem(ctx, 2)
        self.x, self.c = fsdp // 2, lax.rem(fsdp, 2)
        self.ctx, self.fsdp = ctx, fsdp
        self.core_peer = (ctx, self.x * 2 + 1 - self.c)
        self.x_peer = (ctx, (1 - self.x) * 2 + self.c)
        self.y_peer = (self.z * 2 + 1 - self.y, fsdp)

    def z_index(self, step):
        return lax.rem(self.z + step, self.zn)

    def z_peer(self, step):
        return (self.z_index(step) * 2 + self.y, self.fsdp)


def greet(peers):
    barrier = pltpu.get_barrier_semaphore()
    for peer in peers:
        pl.semaphore_signal(barrier, inc=1, device_id=peer, device_id_type=MESH)
    pl.semaphore_wait(barrier, len(peers))


class Sender:
    def __init__(self, send_sem, recv_sem):
        self.send_sem, self.recv_sem = send_sem, recv_sem
        self.used = 0
        self.copies = []

    def start(self, source, target, peer):
        slot = self.used
        self.used += 1
        copy = pltpu.make_async_remote_copy(
            src_ref=source,
            dst_ref=target,
            send_sem=self.send_sem.at[slot],
            recv_sem=self.recv_sem.at[slot],
            device_id=peer,
            device_id_type=MESH,
        )
        copy.start()
        self.copies.append(copy)
        return copy

    def finish(self):
        for copy in self.copies:
            copy.wait_send()


def rows_at(start, size):
    return pl.ds(pl.multiple_of(start, 16), size)


def gather_kernel(plan, count, with_kv, zn, *refs):
    total = count + with_kv
    ins, outs = refs[:total], refs[total : 2 * total]
    send_sem, recv_sem, own_sem = refs[2 * total :]
    here = Place(zn)
    peers = [here.core_peer, here.x_peer, here.y_peer]
    greet(peers + [here.z_peer(step) for step in range(1, zn)] * with_kv)
    sender = Sender(send_sem, recv_sem)
    own_copies = []
    if with_kv:
        kv_in, kv_out = ins[count], outs[count]
        along_z = [
            sender.start(kv_in, kv_out.at[here.ctx], here.z_peer(step)) for step in range(1, zn)
        ]
        along_y = [sender.start(kv_in, kv_out.at[here.ctx], here.y_peer)]
        own_kv = pltpu.make_async_copy(kv_in, kv_out.at[here.ctx], own_sem.at[len(plan)])
        own_kv.start()
        own_copies.append(own_kv)
    state = {}

    def spot(chunk, quarter, half):
        index, col, width = chunk
        rows = ins[index].shape[0]
        if half is None:
            return outs[index].at[rows_at(quarter * rows, rows), pl.ds(col, width)]
        return outs[index].at[
            rows_at(quarter * rows + half * (rows // 2), rows // 2), pl.ds(col, width)
        ]

    def stage(level, at):
        chunk = plan[at]
        index, col, width = chunk
        rows = ins[index].shape[0]
        far = (1 - here.x) * 2 + here.c
        if level == 0:
            half = ins[index].at[rows_at(here.y * (rows // 2), rows // 2), pl.ds(col, width)]
            whole = ins[index].at[:, pl.ds(col, width)]
            to_x = sender.start(half, spot(chunk, here.fsdp, here.y), here.x_peer)
            to_core = sender.start(whole, spot(chunk, here.fsdp, None), here.core_peer)
            own = pltpu.make_async_copy(whole, spot(chunk, here.fsdp, None), own_sem.at[at])
            own.start()
            own_copies.append(own)
            state[at] = [to_x, to_core]
        elif level == 1:
            state[at][0].wait_recv()
            block = spot(chunk, far, here.y)
            state[at].append(sender.start(block, block, here.y_peer))
            state[at].append(sender.start(block, block, here.core_peer))
        elif level == 2:
            state[at][2].wait_recv()
            block = spot(chunk, far, 1 - here.y)
            state[at].append(sender.start(block, block, here.core_peer))
        else:
            for part in (1, 3, 4):
                state[at][part].wait_recv()

    for at in range(len(plan)):
        stage(0, at)
    for tick in range(len(plan) + 2):
        for level in (3, 2, 1):
            at = tick - (level - 1)
            if 0 <= at < len(plan):
                stage(level, at)
        if with_kv and tick < zn - 1:
            along_z[tick].wait_recv()
            block = kv_out.at[here.z_index(zn - 1 - tick) * 2 + here.y]
            along_y.append(sender.start(block, block, here.y_peer))
    if with_kv:
        for copy in along_y:
            copy.wait_recv()
    for own in own_copies:
        own.wait()
    sender.finish()


def gather_weights(arrays, kv, zn):
    plan = []
    for index, array in enumerate(arrays):
        width = array.shape[1]
        step = 1024 if width % 1024 == 0 else 768 if width % 768 == 0 else width
        plan += [(index, col, step) for col in range(0, width, step)]
    count = len(arrays)
    assert len(plan) + 2 >= zn - 1
    shapes = [((4 * array.shape[0], array.shape[1]), array.dtype) for array in arrays]
    shapes += [((2 * zn,) + block.shape, block.dtype) for block in kv]
    copies = 5 * len(plan) + len(kv) * (2 * zn - 1)
    return pl.pallas_call(
        functools.partial(gather_kernel, plan, count, len(kv), zn),
        out_shape=[jax.ShapeDtypeStruct(*shape) for shape in shapes],
        in_specs=[pl.BlockSpec(memory_space=pltpu.VMEM)] * (count + len(kv)),
        out_specs=[pl.BlockSpec(memory_space=pltpu.VMEM)] * (count + len(kv)),
        scratch_shapes=[
            pltpu.SemaphoreType.DMA((copies,)),
            pltpu.SemaphoreType.DMA((copies,)),
            pltpu.SemaphoreType.DMA((len(plan) + len(kv),)),
        ],
        compiler_params=pltpu.CompilerParams(
            collective_id=len(kv), has_side_effects=True, vmem_limit_bytes=VMEM_LIMIT
        ),
    )(*arrays, *kv)


def reduce_kernel(plan, count, with_kv, zn, *refs):
    ins, small_in = refs[:count], refs[count]
    outs, small_out = refs[count + 1 : 2 * count + 1], refs[2 * count + 1]
    rest = refs[2 * count + 2 :]
    buffers = [rest[5 * at : 5 * at + 5] for at in range(len(plan))]
    small_recv, small_sum, small_z, send_sem, recv_sem = rest[5 * len(plan) :]
    here = Place(zn)
    greet(
        [here.core_peer, here.x_peer, here.y_peer] + [here.z_peer(step) for step in range(1, zn)]
    )
    sender = Sender(send_sem, recv_sem)
    state = {}
    own = here.fsdp
    away = (1 - here.x) * 2 + here.c

    def piece(chunk, z_at):
        index, row, rows, col, width, by_rows = chunk
        half = rows // 2
        if by_rows:
            return (z_at * (half // zn), half // zn, 0, width)
        return (0, half, z_at * (width // zn), width // zn)

    def cut(ref, chunk, z_at, row_base, col_base):
        r0, rows, c0, width = piece(chunk, z_at)
        return ref.at[
            rows_at(row_base + r0, rows), pl.ds(pl.multiple_of(col_base + c0, 128), width)
        ]

    def block(ref, chunk, quarter):
        index, row, rows, col, width, by_rows = chunk
        whole = ref.shape[0] // 4
        return ref.at[rows_at(quarter * whole + row, rows), pl.ds(col, width)]

    def stage(level, at):
        chunk = plan[at]
        index, row, rows, col, width, by_rows = chunk
        from_core, from_x, total, from_y, from_z = buffers[at]
        half = rows // 2
        mine = rows_at(here.y * half, half)
        other = rows_at((1 - here.y) * half, half)
        if level == 0:
            state[at] = [
                sender.start(
                    block(ins[index], chunk, side * 2 + 1 - here.c),
                    from_core.at[side],
                    here.core_peer,
                )
                for side in (0, 1)
            ]
        elif level == 1:
            for copy in state[at]:
                copy.wait_recv()
            side = 1 - here.x
            from_core[side] = (
                block(ins[index], chunk, away)[...].astype(F32) + from_core[side].astype(F32)
            ).astype(BF)
            state[at] = [sender.start(from_core.at[side], from_x, here.x_peer)]
        elif level == 2:
            state[at][0].wait_recv()
            total[...] = (
                block(ins[index], chunk, own)[...].astype(F32)
                + from_core[here.x].astype(F32)
                + from_x[...].astype(F32)
            ).astype(BF)
            state[at] = [sender.start(total.at[other], from_y, here.y_peer)]
        elif level == 3:
            state[at][0].wait_recv()
            total[mine] = (total[mine].astype(F32) + from_y[...].astype(F32)).astype(BF)
            state[at] = [
                sender.start(
                    cut(total, chunk, here.z_index(step), here.y * half, 0),
                    from_z.at[step - 1],
                    here.z_peer(step),
                )
                for step in range(1, zn)
            ]
        elif level == 4:
            for copy in state[at]:
                copy.wait_recv()
            result = cut(total, chunk, here.z, here.y * half, 0)[...].astype(F32)
            for step in range(1, zn):
                result = result + from_z[step - 1].astype(F32)
            place = cut(outs[index], chunk, here.z, row + here.y * half, col)
            place[...] = result.astype(BF)
            state[at] = [sender.start(place, place, here.z_peer(step)) for step in range(1, zn)]
        elif level == 5:
            for copy in state[at]:
                copy.wait_recv()
            place = outs[index].at[rows_at(row + here.y * half, half), pl.ds(col, width)]
            state[at] = [sender.start(place, place, here.y_peer)]
        else:
            state[at][0].wait_recv()

    def small_stage(level):
        if level == 0:
            state["s"] = [sender.start(small_in, small_recv.at[0], here.core_peer)]
        elif level in (1, 2):
            state["s"][0].wait_recv()
            base = small_in if level == 1 else small_sum.at[0]
            small_sum[level - 1] = base[...] + small_recv[level - 1]
            peer = here.x_peer if level == 1 else here.y_peer
            state["s"] = [sender.start(small_sum.at[level - 1], small_recv.at[level], peer)]
        elif level == 3:
            state["s"][0].wait_recv()
            small_z[here.z] = small_sum[1] + small_recv[2]
            state["s"] = [
                sender.start(small_z.at[here.z], small_z.at[here.z], here.z_peer(step))
                for step in range(1, zn)
            ]
        elif level == 4:
            for copy in state["s"]:
                copy.wait_recv()
            result = small_z[0]
            for z_at in range(1, zn):
                result = result + small_z[z_at]
            small_out[...] = result

    order_z = list(range(1, zn)) + [0]

    def kv_stage(level):
        if level == 0:
            state["y"] = []
            state["z"] = []
            for step in order_z:
                target = here.z_index(step)
                state["y"].append(
                    sender.start(
                        small_in.at[target * 2 + 1 - here.y], small_recv.at[target], here.y_peer
                    )
                )
        elif level == 1:
            for at, step in enumerate(order_z):
                state["y"][at].wait_recv()
                target = here.z_index(step)
                both = small_in[target * 2 + here.y].astype(F32) + small_recv[target].astype(F32)
                if step == 0:
                    small_out[...] = both
                else:
                    small_sum[step - 1] = both.astype(BF)
                    state["z"].append(
                        sender.start(
                            small_sum.at[step - 1], small_z.at[step - 1], here.z_peer(step)
                        )
                    )
        elif level == 4:
            for step in range(1, zn):
                state["z"][step - 1].wait_recv()
                small_out[...] += small_z[step - 1].astype(F32)

    for tick in range(len(plan) + 6):
        for level in range(6, -1, -1):
            at = tick - level
            if 0 <= at < len(plan):
                stage(level, at)
        if tick < 5:
            (kv_stage if with_kv else small_stage)(tick)
    sender.finish()


def reduce_plan(arrays, zn):
    plan = []
    for index, array in enumerate(arrays):
        rows, width = array.shape[0] // 4, array.shape[1]
        if width % (128 * zn) == 0:
            step = 128 * zn
            cols = list(range(0, width, step))
            if len(cols) >= 6:
                cols = [0] + cols[1:-1:2] + [width - step]
            ends = cols[1:] + [width]
            plan += [
                (index, 0, rows, col, end - col, False) for col, end in zip(cols, ends)
            ]
        else:
            step = 256 if rows % 256 == 0 else rows
            plan += [(index, row, step, 0, width, True) for row in range(0, rows, step)]
    wide = [at for at, chunk in enumerate(plan) if not chunk[5]]
    if wide:
        plan = [plan[wide[0]]] + plan[: wide[0]] + plan[wide[0] + 1 :]
    return plan


def reduce_weights(arrays, small, with_kv, zn):
    plan = reduce_plan(arrays, zn)
    count = len(arrays)
    scratch = []
    for index, row, rows, col, width, by_rows in plan:
        half = rows // 2
        z_shape = (half // zn, width) if by_rows else (half, width // zn)
        scratch += [
            pltpu.VMEM((2, rows, width), BF),
            pltpu.VMEM((rows, width), BF),
            pltpu.VMEM((rows, width), BF),
            pltpu.VMEM((half, width), BF),
            pltpu.VMEM((zn - 1,) + z_shape, BF),
        ]
    copies = len(plan) * (5 + 2 * (zn - 1)) + 2 * zn + 2
    if with_kv:
        shape = small.shape[1:]
        scratch += [
            pltpu.VMEM((zn,) + shape, BF),
            pltpu.VMEM((zn - 1,) + shape, BF),
            pltpu.VMEM((zn - 1,) + shape, BF),
        ]
    else:
        shape = small.shape
        scratch += [
            pltpu.VMEM((3,) + shape, F32),
            pltpu.VMEM((2,) + shape, F32),
            pltpu.VMEM((zn,) + shape, F32),
        ]
    return pl.pallas_call(
        functools.partial(reduce_kernel, plan, count, with_kv, zn),
        out_shape=[
            jax.ShapeDtypeStruct((array.shape[0] // 4, array.shape[1]), array.dtype)
            for array in arrays
        ]
        + [jax.ShapeDtypeStruct(shape, F32)],
        in_specs=[pl.BlockSpec(memory_space=pltpu.VMEM)] * (count + 1),
        out_specs=[pl.BlockSpec(memory_space=pltpu.VMEM)] * (count + 1),
        scratch_shapes=scratch
        + [
            pltpu.SemaphoreType.DMA((copies,)),
            pltpu.SemaphoreType.DMA((copies,)),
        ],
        compiler_params=pltpu.CompilerParams(
            collective_id=2 + with_kv, has_side_effects=True, vmem_limit_bytes=VMEM_LIMIT
        ),
    )(*arrays, small)


def shards(
    ctx_count,
    fsdp_count,
    tokens,
    positions,
    qkv_weight,
    out_weight,
    gate_up_weight,
    down_weight,
    norm_gains,
    qk_gains,
    cotangent,
):
    zn = ctx_count // 2
    own_kernels = fsdp_count == 4 and ctx_count == 8
    row_count = tokens.shape[1]
    all_places = positions[0]
    length = all_places.shape[0]
    places = lax.dynamic_slice_in_dim(all_places, lax.axis_index("ctx") * row_count, row_count, 0)
    weights = (out_weight, down_weight, gate_up_weight)
    if own_kernels:
        (qkv_full,) = gather_weights((qkv_weight,), (), zn)
    else:
        qkv_full = lax.all_gather(qkv_weight, "fsdp", axis=0, tiled=True)
    head_size = qk_gains.shape[1]
    query_width = out_weight.shape[0] * fsdp_count
    head_count = query_width // head_size
    hidden_size = down_weight.shape[0] * fsdp_count
    head_scale = head_size ** (-0.5)
    inputs_f = tokens[0].astype(F32)
    normed_in, inv_in = rms_forward(inputs_f, norm_gains[0])
    normed_in_b = normed_in.astype(BF)
    projected = nn(normed_in_b, qkv_full)
    query_pre = projected[:, :query_width].reshape(row_count, head_count, head_size)
    query_pre = query_pre.transpose(1, 0, 2)
    key_pre = projected[:, query_width : query_width + head_size]
    value_b = projected[:, query_width + head_size :].astype(BF)
    cosine, sine_part = rope_tables(places, head_size)
    query_norm, inv_query = rms_forward(query_pre, qk_gains[0])
    key_norm, inv_key = rms_forward(key_pre, qk_gains[1])
    query_b = (rotate(query_norm, cosine, sine_part) * head_scale).astype(BF)
    key_b = rotate(key_norm, cosine, sine_part).astype(BF)
    kv_b = jnp.concatenate([key_b, value_b], 1)
    if own_kernels:
        out_full, down_full, gate_up_full, kv_all = gather_weights(weights, (kv_b,), zn)
        kv_all = kv_all.reshape(length, 2 * head_size)
    else:
        out_full, down_full, gate_up_full = [
            lax.all_gather(weight, "fsdp", axis=0, tiled=True) for weight in weights
        ]
        kv_all = lax.all_gather(kv_b, "ctx", axis=0, tiled=True)
    key_all, value_all = kv_all[:, :head_size], kv_all[:, head_size:]
    query_rows = query_b.reshape(head_count * row_count, head_size)
    row_places = jnp.tile(places, head_count)
    visible = all_places[None, :] <= row_places[:, None]
    scores = jnp.where(visible, nt(query_rows, key_all), NEG)
    row_peak = jnp.max(scores, axis=1, keepdims=True)
    log_total = row_peak + jnp.log(jnp.sum(jnp.exp(scores - row_peak), axis=1, keepdims=True))
    probs_f = jnp.exp(scores - log_total)
    probs_b = probs_f.astype(BF)
    mixed_rows = nn(probs_b, value_all).astype(BF)

    def heads_in(rows):
        return rows.reshape(head_count, row_count, head_size)

    mixed_b = heads_in(mixed_rows).transpose(1, 0, 2).reshape(row_count, query_width)
    attn_out = nn(mixed_b, out_full)
    attn_norm, inv_attn = rms_forward(attn_out, norm_gains[1])
    resid = inputs_f + attn_norm
    normed_ff, inv_ff = rms_forward(resid, norm_gains[2])
    normed_ff_b = normed_ff.astype(BF)
    gate_up = nn(normed_ff_b, gate_up_full)
    gate_part = gate_up[:, :hidden_size]
    up_part = gate_up[:, hidden_size:]
    activated, gelu_pull = jax.vjp(gelu_tanh, gate_part)
    hidden_b = (activated * up_part).astype(BF)
    ffn_out = nn(hidden_b, down_full)
    ffn_norm, inv_out = rms_forward(ffn_out, norm_gains[3])
    output = resid + ffn_norm
    grad_f = cotangent[0].astype(F32)
    d_ffn, gain_three = rms_backward(ffn_out, inv_out, norm_gains[3], grad_f)
    d_ffn_b = d_ffn.astype(BF)
    grad_down_full = tn(hidden_b, d_ffn_b).astype(BF)
    d_hidden = nt(d_ffn_b, down_full)
    d_gate = gelu_pull(d_hidden * up_part)[0]
    d_gate_up_b = jnp.concatenate([d_gate, d_hidden * activated], 1).astype(BF)
    grad_gate_up_full = tn(normed_ff_b, d_gate_up_b).astype(BF)
    d_normed_ff = nt(d_gate_up_b, gate_up_full)
    d_resid_part, gain_two = rms_backward(resid, inv_ff, norm_gains[2], d_normed_ff)
    d_resid = grad_f + d_resid_part
    d_attn, gain_one = rms_backward(attn_out, inv_attn, norm_gains[1], d_resid)
    d_attn_b = d_attn.astype(BF)
    grad_out_full = tn(mixed_b, d_attn_b).astype(BF)
    d_mixed_b = nt(d_attn_b, out_full).astype(BF)
    d_mixed_rows = d_mixed_b.reshape(row_count, head_count, head_size).transpose(1, 0, 2)
    d_mixed_rows = d_mixed_rows.reshape(head_count * row_count, head_size)
    row_delta = jnp.sum(
        d_mixed_rows.astype(F32) * mixed_rows.astype(F32), axis=-1, keepdims=True
    )
    value_acc = tn(probs_b, d_mixed_rows)
    grad_probs = nt(d_mixed_rows, value_all)
    grad_scores = (probs_f * (grad_probs - row_delta)).astype(BF)
    d_query = heads_in(nn(grad_scores, key_all))
    key_acc = tn(grad_scores, query_rows)
    kv_acc = jnp.concatenate([key_acc, value_acc], 1)
    if own_kernels:
        kv_parts = kv_acc.astype(BF).reshape(2 * zn, row_count, 2 * head_size)
        grads = (grad_down_full, grad_out_full, grad_gate_up_full)
        grad_down, grad_out, grad_gate_up, kv_grad = reduce_weights(grads, kv_parts, 1, zn)
    else:
        kv_grad = lax.psum_scatter(kv_acc, "ctx", scatter_dimension=0, tiled=True)
    d_query_norm = rotate(d_query * head_scale, cosine, -sine_part)
    d_query_pre, gain_query = rms_backward(query_pre, inv_query, qk_gains[0], d_query_norm)
    d_key_norm = rotate(kv_grad[:, :head_size], cosine, -sine_part)
    d_key_pre, gain_key = rms_backward(key_pre, inv_key, qk_gains[1], d_key_norm)
    d_query_flat = d_query_pre.transpose(1, 0, 2).reshape(row_count, query_width)
    d_projected_b = jnp.concatenate([d_query_flat, d_key_pre, kv_grad[:, head_size:]], 1)
    d_projected_b = d_projected_b.astype(BF)
    grad_qkv_full = tn(normed_in_b, d_projected_b).astype(BF)
    d_normed_in = nt(d_projected_b, qkv_full)
    d_inputs, gain_zero = rms_backward(inputs_f, inv_in, norm_gains[0], d_normed_in)
    grad_tokens = d_resid + d_inputs
    gains_local = jnp.stack([gain_zero, gain_one, gain_two, gain_three], 0)
    qk_local = jnp.stack([gain_query, gain_key], 0)
    if own_kernels:
        wide = norm_gains.shape[1] - head_size
        small = jnp.concatenate(
            [gains_local, jnp.pad(qk_local, ((0, 2), (0, wide)))], 0
        )
        grad_qkv, small = reduce_weights((grad_qkv_full,), small, 0, zn)
        gains_total, qk_total = small[:4], small[4:6, :head_size]
    else:
        grads = (grad_down_full, grad_gate_up_full, grad_out_full, grad_qkv_full)
        parts = [lax.psum_scatter(grad, "fsdp", scatter_dimension=0, tiled=True) for grad in grads]
        parts = lax.psum([part.astype(F32) for part in parts], "ctx")
        grad_down, grad_gate_up, grad_out, grad_qkv = parts
        gains_total, qk_total = lax.psum((gains_local, qk_local), ("ctx", "fsdp"))
    return (
        output[None],
        grad_tokens[None],
        grad_qkv.astype(F32),
        grad_out.astype(F32),
        grad_gate_up.astype(F32),
        grad_down.astype(F32),
        gains_total,
        qk_total,
    )


def solution(mesh):
    in_specs = (
        P("fsdp", "ctx", None),
        P("fsdp", None),
        P("fsdp", None),
        P("fsdp", None),
        P("fsdp", None),
        P("fsdp", None),
        P(),
        P(),
        P("fsdp", "ctx", None),
    )
    out_specs = (
        P("fsdp", "ctx", None),
        P("fsdp", "ctx", None),
        P("fsdp", None),
        P("fsdp", None),
        P("fsdp", None),
        P("fsdp", None),
        P(),
        P(),
    )
    body = functools.partial(shards, mesh.shape["ctx"], mesh.shape["fsdp"])
    return jax.shard_map(body, mesh=mesh, in_specs=in_specs, out_specs=out_specs, check_vma=False)
```

```python
import functools

import jax
import jax.numpy as jnp
from jax import lax
from jax.experimental import pallas as pl
from jax.experimental.pallas import tpu as pltpu
from jax.sharding import PartitionSpec as P

EPS = 1e-06
ROPE_BASE = 1000000.0
NEG = -1e30
BF = jnp.bfloat16
F32 = jnp.float32
MESH = pl.DeviceIdType.MESH
VMEM_LIMIT = 60 * 1024 * 1024


def rms_forward(entries, weight):
    inv_rms = lax.rsqrt(jnp.mean(entries * entries, axis=-1, keepdims=True) + EPS)
    return (entries * inv_rms * (1.0 + weight), inv_rms)


def rms_backward(entries, inv_rms, weight, incoming):
    normed = entries * inv_rms
    scaled = incoming * (1.0 + weight)
    lead_axes = tuple(range(incoming.ndim - 1))
    d_weight = jnp.sum(incoming * normed, axis=lead_axes)
    d_entries = inv_rms * (scaled - normed * jnp.mean(scaled * normed, axis=-1, keepdims=True))
    return (d_entries, d_weight)


def rope_tables(places, head_size):
    half_size = head_size // 2
    frequency = ROPE_BASE ** (-2.0 * jnp.arange(half_size, dtype=jnp.float32) / head_size)
    angles = places.astype(jnp.float32)[:, None] * frequency[None, :]
    cosine = jnp.cos(angles)
    sine_part = jnp.sin(angles)
    return (jnp.concatenate([cosine, cosine], -1), jnp.concatenate([sine_part, sine_part], -1))


def rotate(entries, cosine, sine_part):
    half_size = entries.shape[-1] // 2
    turned = jnp.concatenate([-entries[..., half_size:], entries[..., :half_size]], -1)
    return entries * cosine + turned * sine_part


def gelu_tanh(entries):
    return jax.nn.gelu(entries, approximate=True)


def nt(left, right):
    return lax.dot_general(left, right, (((1,), (1,)), ((), ())), preferred_element_type=F32)


def tn(left, right):
    return lax.dot_general(left, right, (((0,), (0,)), ((), ())), preferred_element_type=F32)


def nn(left, right):
    return jnp.dot(left, right, preferred_element_type=F32)


class Place:
    def __init__(self, zn):
        ctx, fsdp = lax.axis_index("ctx"), lax.axis_index("fsdp")
        self.zn = zn
        self.z, self.y = ctx // 2, lax.rem(ctx, 2)
        self.x, self.c = fsdp // 2, lax.rem(fsdp, 2)
        self.ctx, self.fsdp = ctx, fsdp
        self.core_peer = (ctx, self.x * 2 + 1 - self.c)
        self.x_peer = (ctx, (1 - self.x) * 2 + self.c)
        self.y_peer = (self.z * 2 + 1 - self.y, fsdp)

    def z_index(self, step):
        return lax.rem(self.z + step, self.zn)

    def z_peer(self, step):
        return (self.z_index(step) * 2 + self.y, self.fsdp)


def greet(peers):
    barrier = pltpu.get_barrier_semaphore()
    for peer in peers:
        pl.semaphore_signal(barrier, inc=1, device_id=peer, device_id_type=MESH)
    pl.semaphore_wait(barrier, len(peers))


class Sender:
    def __init__(self, send_sem, recv_sem):
        self.send_sem, self.recv_sem = send_sem, recv_sem
        self.used = 0
        self.copies = []

    def start(self, source, target, peer):
        slot = self.used
        self.used += 1
        copy = pltpu.make_async_remote_copy(
            src_ref=source,
            dst_ref=target,
            send_sem=self.send_sem.at[slot],
            recv_sem=self.recv_sem.at[slot],
            device_id=peer,
            device_id_type=MESH,
        )
        copy.start()
        self.copies.append(copy)
        return copy

    def finish(self):
        for copy in self.copies:
            copy.wait_send()


def rows_at(start, size):
    return pl.ds(pl.multiple_of(start, 16), size)


def gather_kernel(plan, count, with_kv, zn, *refs):
    total = count + with_kv
    ins, outs = refs[:total], refs[total : 2 * total]
    send_sem, recv_sem, own_sem = refs[2 * total :]
    here = Place(zn)
    peers = [here.core_peer, here.x_peer, here.y_peer]
    greet(peers + [here.z_peer(step) for step in range(1, zn)] * with_kv)
    sender = Sender(send_sem, recv_sem)
    own_copies = []
    if with_kv:
        kv_in, kv_out = ins[count], outs[count]
        along_z = [
            sender.start(kv_in, kv_out.at[here.ctx], here.z_peer(step)) for step in range(1, zn)
        ]
        along_y = [sender.start(kv_in, kv_out.at[here.ctx], here.y_peer)]
        own_kv = pltpu.make_async_copy(kv_in, kv_out.at[here.ctx], own_sem.at[len(plan)])
        own_kv.start()
        own_copies.append(own_kv)
    state = {}

    def spot(chunk, quarter, half):
        index, col, width = chunk
        rows = ins[index].shape[0]
        if half is None:
            return outs[index].at[rows_at(quarter * rows, rows), pl.ds(col, width)]
        return outs[index].at[
            rows_at(quarter * rows + half * (rows // 2), rows // 2), pl.ds(col, width)
        ]

    def stage(level, at):
        chunk = plan[at]
        index, col, width = chunk
        rows = ins[index].shape[0]
        far = (1 - here.x) * 2 + here.c
        if level == 0:
            half = ins[index].at[rows_at(here.y * (rows // 2), rows // 2), pl.ds(col, width)]
            whole = ins[index].at[:, pl.ds(col, width)]
            to_x = sender.start(half, spot(chunk, here.fsdp, here.y), here.x_peer)
            to_core = sender.start(whole, spot(chunk, here.fsdp, None), here.core_peer)
            own = pltpu.make_async_copy(whole, spot(chunk, here.fsdp, None), own_sem.at[at])
            own.start()
            own_copies.append(own)
            state[at] = [to_x, to_core]
        elif level == 1:
            state[at][0].wait_recv()
            block = spot(chunk, far, here.y)
            state[at].append(sender.start(block, block, here.y_peer))
            state[at].append(sender.start(block, block, here.core_peer))
        elif level == 2:
            state[at][2].wait_recv()
            block = spot(chunk, far, 1 - here.y)
            state[at].append(sender.start(block, block, here.core_peer))
        else:
            for part in (1, 3, 4):
                state[at][part].wait_recv()

    for at in range(len(plan)):
        stage(0, at)
    for tick in range(len(plan) + 2):
        for level in (3, 2, 1):
            at = tick - (level - 1)
            if 0 <= at < len(plan):
                stage(level, at)
        if with_kv and tick < zn - 1:
            along_z[tick].wait_recv()
            block = kv_out.at[here.z_index(zn - 1 - tick) * 2 + here.y]
            along_y.append(sender.start(block, block, here.y_peer))
    if with_kv:
        for copy in along_y:
            copy.wait_recv()
    for own in own_copies:
        own.wait()
    sender.finish()


def gather_weights(arrays, kv, zn):
    plan = []
    for index, array in enumerate(arrays):
        width = array.shape[1]
        step = 1024 if width % 1024 == 0 else 768 if width % 768 == 0 else width
        plan += [(index, col, step) for col in range(0, width, step)]
    count = len(arrays)
    assert len(plan) + 2 >= (zn - 1) * len(kv)
    shapes = [((4 * array.shape[0], array.shape[1]), array.dtype) for array in arrays]
    shapes += [((2 * zn,) + block.shape, block.dtype) for block in kv]
    copies = 5 * len(plan) + len(kv) * (2 * zn - 1)
    return pl.pallas_call(
        functools.partial(gather_kernel, plan, count, len(kv), zn),
        out_shape=[jax.ShapeDtypeStruct(*shape) for shape in shapes],
        in_specs=[pl.BlockSpec(memory_space=pltpu.VMEM)] * (count + len(kv)),
        out_specs=[pl.BlockSpec(memory_space=pltpu.VMEM)] * (count + len(kv)),
        scratch_shapes=[
            pltpu.SemaphoreType.DMA((copies,)),
            pltpu.SemaphoreType.DMA((copies,)),
            pltpu.SemaphoreType.DMA((len(plan) + len(kv),)),
        ],
        compiler_params=pltpu.CompilerParams(
            collective_id=len(kv), has_side_effects=True, vmem_limit_bytes=VMEM_LIMIT
        ),
    )(*arrays, *kv)


def reduce_kernel(plan, count, with_kv, zn, *refs):
    ins, small_in = refs[:count], refs[count]
    outs, small_out = refs[count + 1 : 2 * count + 1], refs[2 * count + 1]
    rest = refs[2 * count + 2 :]
    buffers = [rest[5 * at : 5 * at + 5] for at in range(len(plan))]
    small_recv, small_sum, small_z, send_sem, recv_sem = rest[5 * len(plan) :]
    here = Place(zn)
    greet(
        [here.core_peer, here.x_peer, here.y_peer] + [here.z_peer(step) for step in range(1, zn)]
    )
    sender = Sender(send_sem, recv_sem)
    state = {}
    own = here.fsdp
    away = (1 - here.x) * 2 + here.c

    def piece(chunk, z_at):
        index, row, rows, col, width, by_rows = chunk
        half = rows // 2
        if by_rows:
            return (z_at * (half // zn), half // zn, 0, width)
        return (0, half, z_at * (width // zn), width // zn)

    def cut(ref, chunk, z_at, row_base, col_base):
        r0, rows, c0, width = piece(chunk, z_at)
        return ref.at[
            rows_at(row_base + r0, rows), pl.ds(pl.multiple_of(col_base + c0, 128), width)
        ]

    def block(ref, chunk, quarter):
        index, row, rows, col, width, by_rows = chunk
        whole = ref.shape[0] // 4
        return ref.at[rows_at(quarter * whole + row, rows), pl.ds(col, width)]

    def stage(level, at):
        chunk = plan[at]
        index, row, rows, col, width, by_rows = chunk
        from_core, from_x, total, from_y, from_z = buffers[at]
        half = rows // 2
        mine = rows_at(here.y * half, half)
        other = rows_at((1 - here.y) * half, half)
        if level == 0:
            state[at] = [
                sender.start(
                    block(ins[index], chunk, side * 2 + 1 - here.c),
                    from_core.at[side],
                    here.core_peer,
                )
                for side in (0, 1)
            ]
        elif level == 1:
            for copy in state[at]:
                copy.wait_recv()
            side = 1 - here.x
            from_core[side] = (
                block(ins[index], chunk, away)[...].astype(F32) + from_core[side].astype(F32)
            ).astype(BF)
            state[at] = [sender.start(from_core.at[side], from_x, here.x_peer)]
        elif level == 2:
            state[at][0].wait_recv()
            total[...] = (
                block(ins[index], chunk, own)[...].astype(F32)
                + from_core[here.x].astype(F32)
                + from_x[...].astype(F32)
            ).astype(BF)
            state[at] = [sender.start(total.at[other], from_y, here.y_peer)]
        elif level == 3:
            state[at][0].wait_recv()
            total[mine] = (total[mine].astype(F32) + from_y[...].astype(F32)).astype(BF)
            state[at] = [
                sender.start(
                    cut(total, chunk, here.z_index(step), here.y * half, 0),
                    from_z.at[step - 1],
                    here.z_peer(step),
                )
                for step in range(1, zn)
            ]
        elif level == 4:
            for copy in state[at]:
                copy.wait_recv()
            result = cut(total, chunk, here.z, here.y * half, 0)[...].astype(F32)
            for step in range(1, zn):
                result = result + from_z[step - 1].astype(F32)
            place = cut(outs[index], chunk, here.z, row + here.y * half, col)
            place[...] = result.astype(BF)
            state[at] = [sender.start(place, place, here.z_peer(step)) for step in range(1, zn)]
        elif level == 5:
            for copy in state[at]:
                copy.wait_recv()
            place = outs[index].at[rows_at(row + here.y * half, half), pl.ds(col, width)]
            state[at] = [sender.start(place, place, here.y_peer)]
        else:
            state[at][0].wait_recv()

    def small_stage(level):
        if level == 0:
            state["s"] = [sender.start(small_in, small_recv.at[0], here.core_peer)]
        elif level in (1, 2):
            state["s"][0].wait_recv()
            base = small_in if level == 1 else small_sum.at[0]
            small_sum[level - 1] = base[...] + small_recv[level - 1]
            peer = here.x_peer if level == 1 else here.y_peer
            state["s"] = [sender.start(small_sum.at[level - 1], small_recv.at[level], peer)]
        elif level == 3:
            state["s"][0].wait_recv()
            small_z[here.z] = small_sum[1] + small_recv[2]
            state["s"] = [
                sender.start(small_z.at[here.z], small_z.at[here.z], here.z_peer(step))
                for step in range(1, zn)
            ]
        elif level == 4:
            for copy in state["s"]:
                copy.wait_recv()
            result = small_z[0]
            for z_at in range(1, zn):
                result = result + small_z[z_at]
            small_out[...] = result

    order_z = list(range(1, zn)) + [0]

    def kv_stage(level):
        if level == 0:
            state["y"] = []
            state["z"] = []
            for step in order_z:
                target = here.z_index(step)
                state["y"].append(
                    sender.start(
                        small_in.at[target * 2 + 1 - here.y], small_recv.at[target], here.y_peer
                    )
                )
        elif level == 1:
            for at, step in enumerate(order_z):
                state["y"][at].wait_recv()
                target = here.z_index(step)
                both = small_in[target * 2 + here.y].astype(F32) + small_recv[target].astype(F32)
                if step == 0:
                    small_out[...] = both
                else:
                    small_sum[step - 1] = both.astype(BF)
                    state["z"].append(
                        sender.start(
                            small_sum.at[step - 1], small_z.at[step - 1], here.z_peer(step)
                        )
                    )
        elif level == 4:
            for step in range(1, zn):
                state["z"][step - 1].wait_recv()
                small_out[...] += small_z[step - 1].astype(F32)

    for tick in range(len(plan) + 6):
        for level in range(6, -1, -1):
            at = tick - level
            if 0 <= at < len(plan):
                stage(level, at)
        if tick < 5:
            (kv_stage if with_kv else small_stage)(tick)
    sender.finish()


def reduce_plan(arrays, zn):
    plan = []
    for index, array in enumerate(arrays):
        rows, width = array.shape[0] // 4, array.shape[1]
        if width % (128 * zn) == 0:
            step = 128 * zn
            cols = list(range(0, width, step))
            if len(cols) >= 6:
                cols = [0] + cols[1:-1:2] + [width - step]
            ends = cols[1:] + [width]
            plan += [
                (index, 0, rows, col, end - col, False) for col, end in zip(cols, ends)
            ]
        else:
            step = 256 if rows % 256 == 0 else rows
            plan += [(index, row, step, 0, width, True) for row in range(0, rows, step)]
    wide = [at for at, chunk in enumerate(plan) if not chunk[5]]
    if wide:
        plan = [plan[wide[0]]] + plan[: wide[0]] + plan[wide[0] + 1 :]
    return plan


def reduce_weights(arrays, small, with_kv, zn):
    plan = reduce_plan(arrays, zn)
    count = len(arrays)
    scratch = []
    for index, row, rows, col, width, by_rows in plan:
        half = rows // 2
        z_shape = (half // zn, width) if by_rows else (half, width // zn)
        scratch += [
            pltpu.VMEM((2, rows, width), BF),
            pltpu.VMEM((rows, width), BF),
            pltpu.VMEM((rows, width), BF),
            pltpu.VMEM((half, width), BF),
            pltpu.VMEM((zn - 1,) + z_shape, BF),
        ]
    copies = len(plan) * (5 + 2 * (zn - 1)) + 2 * zn + 2
    if with_kv:
        shape = small.shape[1:]
        scratch += [
            pltpu.VMEM((zn,) + shape, BF),
            pltpu.VMEM((zn - 1,) + shape, BF),
            pltpu.VMEM((zn - 1,) + shape, BF),
        ]
    else:
        shape = small.shape
        scratch += [
            pltpu.VMEM((3,) + shape, F32),
            pltpu.VMEM((2,) + shape, F32),
            pltpu.VMEM((zn,) + shape, F32),
        ]
    return pl.pallas_call(
        functools.partial(reduce_kernel, plan, count, with_kv, zn),
        out_shape=[
            jax.ShapeDtypeStruct((array.shape[0] // 4, array.shape[1]), array.dtype)
            for array in arrays
        ]
        + [jax.ShapeDtypeStruct(shape, F32)],
        in_specs=[pl.BlockSpec(memory_space=pltpu.VMEM)] * (count + 1),
        out_specs=[pl.BlockSpec(memory_space=pltpu.VMEM)] * (count + 1),
        scratch_shapes=scratch
        + [
            pltpu.SemaphoreType.DMA((copies,)),
            pltpu.SemaphoreType.DMA((copies,)),
        ],
        compiler_params=pltpu.CompilerParams(
            collective_id=2 + with_kv, has_side_effects=True, vmem_limit_bytes=VMEM_LIMIT
        ),
    )(*arrays, small)


def shards(
    ctx_count,
    fsdp_count,
    tokens,
    positions,
    qkv_weight,
    out_weight,
    gate_up_weight,
    down_weight,
    norm_gains,
    qk_gains,
    cotangent,
):
    zn = ctx_count // 2
    own_kernels = fsdp_count == 4 and ctx_count == 8
    row_count = tokens.shape[1]
    all_places = positions[0]
    length = all_places.shape[0]
    places = lax.dynamic_slice_in_dim(all_places, lax.axis_index("ctx") * row_count, row_count, 0)
    weights = (out_weight, down_weight)
    gate_up_full = lax.all_gather(gate_up_weight, "fsdp", axis=0, tiled=True)
    if own_kernels:
        (qkv_full,) = gather_weights((qkv_weight,), (), zn)
    else:
        qkv_full = lax.all_gather(qkv_weight, "fsdp", axis=0, tiled=True)
    head_size = qk_gains.shape[1]
    query_width = out_weight.shape[0] * fsdp_count
    head_count = query_width // head_size
    hidden_size = down_weight.shape[0] * fsdp_count
    head_scale = head_size ** (-0.5)
    inputs_f = tokens[0].astype(F32)
    normed_in, inv_in = rms_forward(inputs_f, norm_gains[0])
    normed_in_b = normed_in.astype(BF)
    projected = nn(normed_in_b, qkv_full)
    query_pre = projected[:, :query_width].reshape(row_count, head_count, head_size)
    query_pre = query_pre.transpose(1, 0, 2)
    key_pre = projected[:, query_width : query_width + head_size]
    value_b = projected[:, query_width + head_size :].astype(BF)
    cosine, sine_part = rope_tables(places, head_size)
    query_norm, inv_query = rms_forward(query_pre, qk_gains[0])
    key_norm, inv_key = rms_forward(key_pre, qk_gains[1])
    query_b = (rotate(query_norm, cosine, sine_part) * head_scale).astype(BF)
    key_b = rotate(key_norm, cosine, sine_part).astype(BF)
    kv_b = jnp.concatenate([key_b, value_b], 1)
    if own_kernels:
        out_full, down_full, kv_all = gather_weights(weights, (kv_b,), zn)
        kv_all = kv_all.reshape(length, 2 * head_size)
    else:
        out_full, down_full = [
            lax.all_gather(weight, "fsdp", axis=0, tiled=True) for weight in weights
        ]
        kv_all = lax.all_gather(kv_b, "ctx", axis=0, tiled=True)
    key_all, value_all = kv_all[:, :head_size], kv_all[:, head_size:]
    query_rows = query_b.reshape(head_count * row_count, head_size)
    row_places = jnp.tile(places, head_count)
    visible = all_places[None, :] <= row_places[:, None]
    scores = jnp.where(visible, nt(query_rows, key_all), NEG)
    row_peak = jnp.max(scores, axis=1, keepdims=True)
    log_total = row_peak + jnp.log(jnp.sum(jnp.exp(scores - row_peak), axis=1, keepdims=True))
    probs_f = jnp.exp(scores - log_total)
    probs_b = probs_f.astype(BF)
    mixed_rows = nn(probs_b, value_all).astype(BF)

    def heads_in(rows):
        return rows.reshape(head_count, row_count, head_size)

    mixed_b = heads_in(mixed_rows).transpose(1, 0, 2).reshape(row_count, query_width)
    attn_out = nn(mixed_b, out_full)
    attn_norm, inv_attn = rms_forward(attn_out, norm_gains[1])
    resid = inputs_f + attn_norm
    normed_ff, inv_ff = rms_forward(resid, norm_gains[2])
    normed_ff_b = normed_ff.astype(BF)
    gate_up = nn(normed_ff_b, gate_up_full)
    gate_part = gate_up[:, :hidden_size]
    up_part = gate_up[:, hidden_size:]
    activated, gelu_pull = jax.vjp(gelu_tanh, gate_part)
    hidden_b = (activated * up_part).astype(BF)
    ffn_out = nn(hidden_b, down_full)
    ffn_norm, inv_out = rms_forward(ffn_out, norm_gains[3])
    output = resid + ffn_norm
    grad_f = cotangent[0].astype(F32)
    d_ffn, gain_three = rms_backward(ffn_out, inv_out, norm_gains[3], grad_f)
    d_ffn_b = d_ffn.astype(BF)
    grad_down_full = tn(hidden_b, d_ffn_b).astype(BF)
    d_hidden = nt(d_ffn_b, down_full)
    d_gate = gelu_pull(d_hidden * up_part)[0]
    d_gate_up_b = jnp.concatenate([d_gate, d_hidden * activated], 1).astype(BF)
    grad_gate_up_full = tn(normed_ff_b, d_gate_up_b).astype(BF)
    d_normed_ff = nt(d_gate_up_b, gate_up_full)
    d_resid_part, gain_two = rms_backward(resid, inv_ff, norm_gains[2], d_normed_ff)
    d_resid = grad_f + d_resid_part
    d_attn, gain_one = rms_backward(attn_out, inv_attn, norm_gains[1], d_resid)
    d_attn_b = d_attn.astype(BF)
    grad_out_full = tn(mixed_b, d_attn_b).astype(BF)
    d_mixed_b = nt(d_attn_b, out_full).astype(BF)
    d_mixed_rows = d_mixed_b.reshape(row_count, head_count, head_size).transpose(1, 0, 2)
    d_mixed_rows = d_mixed_rows.reshape(head_count * row_count, head_size)
    row_delta = jnp.sum(
        d_mixed_rows.astype(F32) * mixed_rows.astype(F32), axis=-1, keepdims=True
    )
    value_acc = tn(probs_b, d_mixed_rows)
    grad_probs = nt(d_mixed_rows, value_all)
    grad_scores = (probs_f * (grad_probs - row_delta)).astype(BF)
    d_query = heads_in(nn(grad_scores, key_all))
    key_acc = tn(grad_scores, query_rows)
    kv_acc = jnp.concatenate([key_acc, value_acc], 1)
    if own_kernels:
        kv_parts = kv_acc.astype(BF).reshape(2 * zn, row_count, 2 * head_size)
        grads = (grad_down_full, grad_out_full, grad_gate_up_full)
        grad_down, grad_out, grad_gate_up, kv_grad = reduce_weights(grads, kv_parts, 1, zn)
    else:
        kv_grad = lax.psum_scatter(kv_acc, "ctx", scatter_dimension=0, tiled=True)
    d_query_norm = rotate(d_query * head_scale, cosine, -sine_part)
    d_query_pre, gain_query = rms_backward(query_pre, inv_query, qk_gains[0], d_query_norm)
    d_key_norm = rotate(kv_grad[:, :head_size], cosine, -sine_part)
    d_key_pre, gain_key = rms_backward(key_pre, inv_key, qk_gains[1], d_key_norm)
    d_query_flat = d_query_pre.transpose(1, 0, 2).reshape(row_count, query_width)
    d_projected_b = jnp.concatenate([d_query_flat, d_key_pre, kv_grad[:, head_size:]], 1)
    d_projected_b = d_projected_b.astype(BF)
    grad_qkv_full = tn(normed_in_b, d_projected_b).astype(BF)
    d_normed_in = nt(d_projected_b, qkv_full)
    d_inputs, gain_zero = rms_backward(inputs_f, inv_in, norm_gains[0], d_normed_in)
    grad_tokens = d_resid + d_inputs
    gains_local = jnp.stack([gain_zero, gain_one, gain_two, gain_three], 0)
    qk_local = jnp.stack([gain_query, gain_key], 0)
    if own_kernels:
        wide = norm_gains.shape[1] - head_size
        small = jnp.concatenate(
            [gains_local, jnp.pad(qk_local, ((0, 2), (0, wide)))], 0
        )
        grad_qkv, small = reduce_weights((grad_qkv_full,), small, 0, zn)
        gains_total, qk_total = small[:4], small[4:6, :head_size]
    else:
        grads = (grad_down_full, grad_gate_up_full, grad_out_full, grad_qkv_full)
        parts = [lax.psum_scatter(grad, "fsdp", scatter_dimension=0, tiled=True) for grad in grads]
        parts = lax.psum([part.astype(F32) for part in parts], "ctx")
        grad_down, grad_gate_up, grad_out, grad_qkv = parts
        gains_total, qk_total = lax.psum((gains_local, qk_local), ("ctx", "fsdp"))
    return (
        output[None],
        grad_tokens[None],
        grad_qkv.astype(F32),
        grad_out.astype(F32),
        grad_gate_up.astype(F32),
        grad_down.astype(F32),
        gains_total,
        qk_total,
    )


def solution(mesh):
    in_specs = (
        P("fsdp", "ctx", None),
        P("fsdp", None),
        P("fsdp", None),
        P("fsdp", None),
        P("fsdp", None),
        P("fsdp", None),
        P(),
        P(),
        P("fsdp", "ctx", None),
    )
    out_specs = (
        P("fsdp", "ctx", None),
        P("fsdp", "ctx", None),
        P("fsdp", None),
        P("fsdp", None),
        P("fsdp", None),
        P("fsdp", None),
        P(),
        P(),
    )
    body = functools.partial(shards, mesh.shape["ctx"], mesh.shape["fsdp"])
    return jax.shard_map(body, mesh=mesh, in_specs=in_specs, out_specs=out_specs, check_vma=False)
```
